256 devices in a mesh: section: 32 (over z_hi, x, core), rep: 8 (over z_lo, y).
Axes of the slice: x: 4, y: 4, z: 8 (z_hi: 4, z_lo: 2; z = z_hi * 2 + z_lo), core: 2. Of those that a mesh axis runs over, the one named last changes fastest.
Arguments:
- features: bfloat16 [65536, 256], P(('section', 'rep')), may hold values from -6 to 6
- tiles: bfloat16 [32, 8, 64, 256, 256], P('section', 'rep'), may hold values from -0.0625 to 0.0625
- tile_rows: int32 [32, 8, 64], P('section', 'rep'), may hold values from 0 to 7, as said below
- tile_cols: int32 [32, 8, 64], P('section', 'rep'), may hold values from 0 to 31, as said below
- tile_count: int32 [32, 8], P('section', 'rep'), may hold values from 16 to 64, as said below
- weight: bfloat16 [256, 256], replicated, may hold values from -0.375 to 0.375
- cotangent: bfloat16 [65536, 256], P(('section', 'rep')), may hold values from -6 to 6
Outputs:
- activated: bfloat16 [65536, 256], P(('section', 'rep'))
- weight_grad: float32 [256, 256], replicated
- feature_grad: bfloat16 [65536, 256], P(('section', 'rep'))
The draws below stay inside these ranges and needn't reach their ends.
Inputs may be any that keep to these rules, and one draw needn't show every extreme that they name: `tile_rows`: on each device the first tile_count slots name distinct pairs of tile row and tile column; slots from tile_count on are unused, whatever they hold. `tile_cols`: tile column within the column set of the device's rep index, which has 32 * 8 / 8 tiles. `tile_count`: some device uses all 64 slots.
All inputs are finite; a program needn't handle non-finite values.
Results may differ from the reference program's by a relative error of at most 0.0065.
Values may be sent and summed in bfloat16 or wider, within the bound.
A program may use at most 128 MiB of HBM per device.

```python
import jax
import jax.numpy as jnp
from jax import lax

F = 256
TILE = 256
RB = 8
SLOTS = 64
NODES = 65536
N_SECTION = 32
N_REP = 8


def place_tiles(key):
    positions = RB * (N_SECTION * RB // N_REP)
    col_tiles = N_SECTION * RB // N_REP
    keys = jax.random.split(key, N_SECTION * N_REP)
    picked = jax.vmap(lambda one_key: jax.random.permutation(one_key, positions)[:SLOTS])(keys)
    picked = picked.reshape(N_SECTION, N_REP, SLOTS).astype(jnp.int32)
    return (picked // col_tiles, picked % col_tiles)


def draw_tile_rows(key, part):
    row_ids, col_ids = place_tiles(key)
    return row_ids


def draw_tile_cols(key, part):
    row_ids, col_ids = place_tiles(key)
    return col_ids


def draw_tile_count(key, part):
    key = jax.random.fold_in(key, 5)
    first_key, second_key = jax.random.split(key)
    divisor = jax.random.randint(first_key, (N_SECTION, N_REP), 1, 5)
    counts = SLOTS // divisor
    busiest = jax.random.randint(second_key, (), 0, N_SECTION * N_REP)
    flat_index = jnp.arange(N_SECTION * N_REP, dtype=jnp.int32).reshape(N_SECTION, N_REP)
    return jnp.where(flat_index == busiest, SLOTS, counts).astype(jnp.int32)


def level_of(key, dims, cuts, low, high):
    def one(dim, blocks):
        draws = jax.random.uniform(jax.random.fold_in(jax.random.fold_in(key, 6), dim), (blocks,), jnp.float32, low / len(cuts), high / len(cuts))
        return jnp.repeat(jnp.exp(draws), dims[dim] // blocks).reshape((-1,) + (1,) * (len(dims) - dim - 1))

    level = one(*cuts[0])
    for cut in cuts[1:]:
        level = level * one(*cut)
    return level


def normal_values(rng, shape, width, most, cuts=(), kind=jnp.bfloat16):
    drawn = width * jax.random.normal(rng, shape, jnp.float32)
    if cuts:
        drawn = drawn * level_of(rng, shape, cuts, -0.22, 0.18)
    return jnp.clip(drawn, -most, most).astype(kind)


def setup_inputs(seed: int = 0) -> dict:
    streams_of = jax.random.split(jax.random.key(seed), 8)
    features = normal_values(streams_of[0], (NODES, F), 1.0, 6.0, ((0, 256),))
    tiles = normal_values(streams_of[1], (N_SECTION, N_REP, SLOTS, TILE, TILE), ((2.0 * RB / (TILE * SLOTS * N_REP)) ** 0.5), 0.0625, ((0, 32), (1, 8)))
    tile_rows = draw_tile_rows(jax.random.fold_in(streams_of[7], 71), 0)
    tile_cols = draw_tile_cols(jax.random.fold_in(streams_of[7], 71), 0)
    tile_count = draw_tile_count(jax.random.fold_in(streams_of[7], 71), 0)
    weight = normal_values(streams_of[5], (F, F), F ** -0.5, 0.375)
    cotangent = normal_values(streams_of[6], (NODES, F), 1.0, 6.0, ((0, 256),))
    return {"features": features, "tiles": tiles, "tile_rows": tile_rows, "tile_cols": tile_cols, "tile_count": tile_count, "weight": weight, "cotangent": cotangent}


def silu_slope(pre_act):
    sigma = jax.nn.sigmoid(pre_act)
    return sigma * (1.0 + pre_act * (1.0 - sigma))


def reference(features, tiles, tile_rows, tile_cols, tile_count, weight, cotangent):
    own_rows = RB * TILE // N_REP
    col_tiles = N_SECTION * own_rows // TILE
    column_sets = jnp.transpose(features.reshape(N_SECTION, N_REP, own_rows, F), (1, 0, 2, 3)).reshape(N_REP, col_tiles, TILE, F)
    slot_index = jnp.arange(SLOTS, dtype=jnp.int32)
    rep_index = jnp.arange(N_REP, dtype=jnp.int32)[:, None]
    row_range = jnp.arange(RB, dtype=jnp.int32)
    col_range = jnp.arange(col_tiles, dtype=jnp.int32)
    cot_blocks = cotangent.reshape(N_SECTION, RB * TILE, F)
    highest = lax.Precision.HIGHEST

    def one_section(carry, inputs):
        grad_sum, sets_grad = carry
        section_tiles, row_ids, col_ids, live_count, section_cot = inputs
        in_use = (slot_index[None, :] < live_count[:, None]).astype(jnp.float32)
        selected = column_sets[rep_index, col_ids]
        tiles_wide = section_tiles.astype(jnp.float32)
        products = jnp.einsum('rkij,rkjf->rkif', tiles_wide, selected.astype(jnp.float32), precision=highest)
        row_hot = (row_ids[..., None] == row_range).astype(jnp.float32) * in_use[..., None]
        aggregate = jnp.einsum('rkt,rkif->tif', row_hot, products, precision=highest).reshape(RB * TILE, F).astype(jnp.bfloat16)
        pre_act = jnp.dot(aggregate, weight, preferred_element_type=jnp.float32)
        activated = jax.nn.silu(pre_act).astype(jnp.bfloat16)
        pre_grad = (section_cot.astype(jnp.float32) * silu_slope(pre_act)).astype(jnp.bfloat16)
        grad_sum = grad_sum + jnp.dot(aggregate.T, pre_grad, preferred_element_type=jnp.float32)
        row_grads = jnp.dot(pre_grad, weight.T, preferred_element_type=jnp.float32).astype(jnp.bfloat16)
        row_grads = lax.optimization_barrier(row_grads)
        chosen = row_grads.reshape(RB, TILE, F)[row_ids]
        backward = jnp.einsum('rkji,rkjf->rkif', tiles_wide, chosen.astype(jnp.float32), precision=highest)
        col_hot = (col_ids[..., None] == col_range).astype(jnp.float32) * in_use[..., None]
        sets_grad = sets_grad + jnp.einsum('rkc,rkif->rcif', col_hot, backward, precision=highest)
        return (grad_sum, sets_grad), activated

    start_carry = (jnp.zeros((F, F), jnp.float32), jnp.zeros((N_REP, col_tiles, TILE, F), jnp.float32))
    (weight_grad, sets_grad), activated = lax.scan(one_section, start_carry, (tiles, tile_rows, tile_cols, tile_count, cot_blocks))
    feature_grad = jnp.transpose(sets_grad.reshape(N_REP, N_SECTION, own_rows, F), (1, 0, 2, 3)).reshape(N_SECTION * N_REP * own_rows, F)
    return activated.reshape(N_SECTION * RB * TILE, F), weight_grad, feature_grad.astype(jnp.bfloat16)
```

```python
import jax
import jax.numpy as jnp
from jax import lax
from jax.experimental import pallas as pl
from jax.experimental.pallas import tpu as pltpu
from jax.sharding import PartitionSpec as P

f32, bf16 = jnp.float32, jnp.bfloat16
T = 256
SLOTS = 64
STEP = (0, 1, -1, 2)
FWD = ((0, 64), (64, 64), (128, 64), (192, 64))
BWD = ((0, 64), (64, 64), (128, 64), (192, 64))
UNROLL = 32


def transpose(v):
    return v.T


def kernel(
    feat_ref, tiles_ref, rows_ref, cols_ref, count_ref, weight_ref, cot_ref,
    act_ref, wgrad_ref, fgrad_ref,
    tiles, tiles_t, prefix, rs_send, rs_recv, agg_own, agg_t, wt, cot_t,
    c_send, c_recv, comb, xh_send, xh_recv, xf_send, xf_recv, z_send, z_recv, fg_t,
    w0, w1r, w1, w2r, w2, w3r, w4, w5, w6, w7, table_v, table,
    send_sem, recv_sem, local_sem, *per_slice,
):
    gathered, row_grads = per_slice[: len(FWD)], per_slice[len(FWD) :]
    section, rep = lax.axis_index("section"), lax.axis_index("rep")
    zh, x, c = section // 8, (section // 2) % 4, section % 2
    zl, y = rep // 4, rep % 4

    def at(dzh=0, dx=0, dc=0, dzl=0, dy=0):
        return (
            (((zh + dzh + 4) % 4) * 4 + (x + dx + 4) % 4) * 2 + (c + dc) % 2,
            ((zl + dzl) % 2) * 4 + (y + dy + 4) % 4,
        )

    rep_offs = [dict(dzl=e // 4, dy=STEP[e % 4]) for e in range(8)]
    partners = (
        [dict(dx=STEP[i]) for i in (1, 2, 3)]
        + [dict(dzh=STEP[i]) for i in (1, 2, 3)]
        + [dict(dc=1)]
        + rep_offs[1:]
    )
    back = (0, 2, 1, 3)
    channels = {}

    def send(key, src, dst, off):
        i = len(channels)
        copy = pltpu.make_async_remote_copy(
            src_ref=src, dst_ref=dst, send_sem=send_sem.at[i], recv_sem=recv_sem.at[i],
            device_id=at(**off), device_id_type=pl.DeviceIdType.MESH,
        )
        copy.start()
        channels[key] = copy

    def recv(key):
        channels[key].wait_recv()

    barrier = pltpu.get_barrier_semaphore()
    for off in partners:
        pl.semaphore_signal(barrier, inc=1, device_id=at(**off), device_id_type=pl.DeviceIdType.MESH)
    loads = [
        pltpu.make_async_copy(tiles_ref.at[pl.ds(i * 8, 8)], tiles.at[pl.ds(i * 8, 8)], local_sem.at[i])
        for i in range(8)
    ]
    for load in loads:
        load.start()
    feat_t = transpose(feat_ref[...])
    for q, (a, n) in enumerate(FWD):
        gathered[q][0] = feat_t[a : a + n]
    pl.semaphore_wait(barrier, len(partners))

    def x_full(q, dz):
        g = gathered[q]
        send(("xf", q, dz, 1), g.at[dz * 4], g.at[dz * 4 + 2], dict(dx=1))
        send(("xf", q, dz, -1), g.at[dz * 4], g.at[dz * 4 + 1], dict(dx=-1))

    for q in range(len(FWD)):
        g = gathered[q]
        for dz in (1, 2, 3):
            send(("z", q, dz), g.at[0], g.at[back[dz] * 4], dict(dzh=STEP[dz]))
        x_full(q, 0)

    def make_tables():
        lane = lax.broadcasted_iota(jnp.int32, (SLOTS, SLOTS), 1)
        sub = lax.broadcasted_iota(jnp.int32, (SLOTS, SLOTS), 0)
        count = count_ref[0, 0]
        r_l = jnp.broadcast_to(rows_ref[...], (SLOTS, SLOTS))
        c_l = jnp.broadcast_to(cols_ref[...], (SLOTS, SLOTS))
        r_s = r_l.astype(f32).T.astype(jnp.int32)
        c_s = c_l.astype(f32).T.astype(jnp.int32)
        live_s = sub < count
        lane_w = lax.broadcasted_iota(jnp.int32, (SLOTS, 128), 1)
        sub_w = lax.broadcasted_iota(jnp.int32, (SLOTS, 128), 0)

        def ring(delta):
            d = (delta + 8) % 4
            return jnp.where(d == 2, 3, jnp.where(d == 3, 2, d))

        def one(major_l, minor_l, major_s, minor_s, width, other, base):
            key_l = jnp.where(lane < count, major_l * width + minor_l, 1000 + lane)
            key_s = jnp.where(live_s, major_s * width + minor_s, 1000 + sub)
            before = key_l < key_s
            rank = jnp.sum(before.astype(f32), axis=1, keepdims=True)
            same = jnp.sum((before & (major_l == major_s)).astype(f32), axis=1, keepdims=True)
            hot = jnp.broadcast_to(rank, (SLOTS, 128)) == lane_w.astype(f32)
            first = jnp.broadcast_to((same == 0).astype(f32), (SLOTS, 128))

            def pick(v):
                return jnp.sum(jnp.where(hot, v, 0.0), axis=0, keepdims=True).astype(jnp.int32)

            major_w = jnp.broadcast_to(major_s[:, :1], (SLOTS, 128))
            live_w = sub_w < count
            upto = jnp.sum((live_w & (major_w <= lane_w)).astype(f32), axis=0, keepdims=True)
            equal = jnp.sum((live_w & (major_w == lane_w)).astype(f32), axis=0, keepdims=True)
            last = jnp.where(equal > 0, upto - 1.0, -1.0).astype(jnp.int32)
            table_v[base : base + 1, :] = pick(sub_w.astype(f32))
            table_v[base + 1 : base + 2, :] = pick(jnp.broadcast_to(other[:, :1].astype(f32), (SLOTS, 128)))
            table_v[base + 2 : base + 3, :] = pick(first)
            table_v[base + 3 : base + 4, :] = last

        where_col = ((c_s + c) % 2) * 16 + ring(c_s // 8 - zh) * 4 + ring((c_s // 2) % 4 - x)
        where_row = ((r_s // 4 + zl) % 2) * 4 + ring(r_s % 4 - y)
        one(r_l, c_l, r_s, c_s, 32, where_col, 0)
        one(c_l, r_l, c_s, r_s, 8, where_row, 4)

    make_tables()
    to_smem = pltpu.make_async_copy(table_v, table, local_sem.at[8])
    to_smem.start()
    for load in loads:
        load.wait()

    def turn(first, number):
        def step(i, carry):
            for u in range(4):
                k = first + i * 4 + u
                tiles_t[k] = transpose(tiles[k])
            return carry

        lax.fori_loop(0, number // 4, step, 0)

    turn(0, 32)
    wt[...] = transpose(weight_ref[...])
    cot_t[...] = transpose(cot_ref[...])

    def products(source, matrices, base, n):
        def step(i, total):
            for u in range(UNROLL):
                p = i * UNROLL + u
                keep = jnp.where(table[base + 2, p] == 1, 0.0, 1.0)
                s = jnp.clip(table[base + 1, p], 0, source.shape[0] - 1)
                k = jnp.clip(table[base, p], 0, SLOTS - 1)
                total = total * keep + jnp.dot(source[s], matrices[k], preferred_element_type=f32)
                prefix[p, :n] = total
            return total

        lax.fori_loop(0, SLOTS // UNROLL, step, jnp.zeros((n, T), f32))

    def group(base, index, n):
        last = table[base + 3, index]
        return prefix[jnp.clip(last, 0, SLOTS - 1), :n] * jnp.where(last >= 0, 1.0, 0.0)

    def stage_x(q):
        g, n = gathered[q], FWD[q][1]
        h = n // 2
        for dz in (1, 2, 3):
            recv(("z", q, dz))
            x_full(q, back[dz])
        for dz in range(4):
            recv(("xf", q, dz, 1))
            send(("xh", q, dz, 1), g.at[dz * 4 + 2, pl.ds(0, h)], g.at[dz * 4 + 3, pl.ds(0, h)], dict(dx=1))
            recv(("xf", q, dz, -1))
            send(("xh", q, dz, -1), g.at[dz * 4 + 1, pl.ds(h, h)], g.at[dz * 4 + 3, pl.ds(h, h)], dict(dx=-1))

    def stage_core(q):
        g = gathered[q]
        for dz in range(4):
            recv(("xh", q, dz, 1))
            recv(("xh", q, dz, -1))
            send(("core", q, dz), g.at[pl.ds(dz * 4, 4)], g.at[pl.ds(16 + dz * 4, 4)], dict(dc=1))

    def stage_products(q):
        a, n = FWD[q]
        for dz in range(4):
            recv(("core", q, dz))
        products(gathered[q], tiles_t, 0, n)
        for e in (7, 3, 6, 5, 2, 1, 4):
            owner = at(**rep_offs[e])[1]
            rs_send[e, a : a + n] = group(0, owner, n).astype(bf16)
            to = (e // 4) * 4 + back[e % 4]
            send(("rs", q, e), rs_send.at[e, pl.ds(a, n)], rs_recv.at[to, pl.ds(a, n)], rep_offs[e])
        agg_own[a : a + n] = group(0, rep, n)

    for q in range(len(FWD) + 1):
        if q < len(FWD):
            stage_x(q)
        if q == 0:
            turn(32, 32)
            to_smem.wait()
        if q >= 1:
            stage_core(q - 1)
            stage_products(q - 1)

    for q, (a, n) in enumerate(FWD):
        for e in range(1, 8):
            recv(("rs", q, e))
        total = agg_own[a : a + n]
        for e in range(1, 8):
            total = total + rs_recv[e, a : a + n].astype(f32)
        agg_t[a : a + n] = total.astype(bf16)

    pre = jnp.dot(wt[...], agg_t[...], preferred_element_type=f32)
    sigma = jax.nn.sigmoid(pre)
    pre_grad = (cot_t[...].astype(f32) * (sigma * (1.0 + pre * (1.0 - sigma)))).astype(bf16)
    for q, (a, n) in enumerate(BWD):
        row_grads[q][0] = jnp.dot(weight_ref[a : a + n], pre_grad, preferred_element_type=f32).astype(bf16)
        for e in (7, 3, 6, 5, 2, 1, 4):
            to = (e // 4) * 4 + back[e % 4]
            send(("ag", q, e), row_grads[q].at[0], row_grads[q].at[to], rep_offs[e])
    act_ref[...] = (pre * sigma).T.astype(bf16)
    w0[...] = lax.dot_general(agg_t[...], pre_grad, (((1,), (1,)), ((), ())), preferred_element_type=f32)

    def aligned(v, k):
        return pl.ds(pl.multiple_of(v * k, k), k)

    def weight_1():
        send("w1", w0.at[aligned(1 - c, 128)], w1r, dict(dc=1))

    def weight_2():
        recv("w1")
        w1[...] = w0[aligned(c, 128), :] + w1r[...]
        for i in (3, 1, 2):
            send(("w2", i), w1.at[aligned((x + STEP[i] + 4) % 4, 32)], w2r.at[back[i] - 1], dict(dx=STEP[i]))

    def weight_3():
        total = w1[aligned(x, 32), :]
        for i in (1, 2, 3):
            recv(("w2", i))
        for i in (1, 2, 3):
            total = total + w2r[i - 1]
        w2[...] = total
        for i in (3, 1, 2):
            send(("w3", i), w2.at[aligned((zh + STEP[i] + 4) % 4, 8)], w3r.at[back[i] - 1], dict(dzh=STEP[i]))

    def weight_4():
        total = w2[aligned(zh, 8), :]
        for i in (1, 2, 3):
            recv(("w3", i))
        for i in (1, 2, 3):
            total = total + w3r[i - 1]
        w4[rep] = total
        for e in range(1, 8):
            send(("w4", e), w4.at[rep], w4.at[rep], rep_offs[e])

    def weight_5():
        for e in range(1, 8):
            recv(("w4", e))
        w5[aligned(zh, 8), :] = jnp.sum(w4[...], axis=0)
        for i in (3, 1, 2):
            send(("w5", i), w5.at[aligned(zh, 8)], w5.at[aligned(zh, 8)], dict(dzh=STEP[i]))

    def weight_6():
        for i in (1, 2, 3):
            recv(("w5", i))
        w6[aligned(x, 32), :] = w5[...]
        for i in (3, 1, 2):
            send(("w6", i), w6.at[aligned(x, 32)], w6.at[aligned(x, 32)], dict(dx=STEP[i]))

    def weight_7():
        for i in (1, 2, 3):
            recv(("w6", i))
        w7[aligned(c, 128), :] = w6[...]
        send("w7", w7.at[aligned(c, 128)], w7.at[aligned(c, 128)], dict(dc=1))

    def weight_8():
        recv("w7")
        wgrad_ref[...] = w7[...]

    def back_products(q):
        a, n = BWD[q]
        for e in range(1, 8):
            recv(("ag", q, e))
        products(row_grads[q], tiles, 4, n)
        for dz in (3, 1, 2, 0):
            for dx in (3, 1, 2, 0):
                other = at(dzh=STEP[dz], dx=STEP[dx], dc=1)[0]
                c_send[dz * 4 + dx, a : a + n] = group(4, other, n).astype(bf16)
            part = (pl.ds(dz * 4, 4), pl.ds(a, n))
            send(("bc", q, dz), c_send.at[part], c_recv.at[part], dict(dc=1))
        for dz in (3, 1, 2, 0):
            for dx in (3, 1, 2, 0):
                own = at(dzh=STEP[dz], dx=STEP[dx])[0]
                comb[dz * 4 + dx, a : a + n] = group(4, own, n)

    def both(i, a, n):
        return comb[i, a : a + n] + c_recv[i, a : a + n].astype(f32)

    def back_xh(q):
        a, n = BWD[q]
        h = n // 2
        for dz in range(4):
            recv(("bc", q, dz))
            xh_send[dz, a : a + n] = both(dz * 4 + 3, a, n).astype(bf16)
        for k, d, s in ((0, 1, a), (1, -1, a + h)):
            send(("bxh", q, k), xh_send.at[:, pl.ds(s, h)], xh_recv.at[:, pl.ds(s, h)], dict(dx=d))

    def back_xf(q):
        a, n = BWD[q]
        h = n // 2
        for k, d, s in ((0, 1, a), (1, -1, a + h)):
            recv(("bxh", q, k))
            o = a + h if k == 0 else a
            for dz in range(4):
                i = dz * 4 + 1 + k
                xf_send[k, dz, s : s + h] = (both(i, s, h) + xh_recv[dz, s : s + h].astype(f32)).astype(bf16)
                xf_send[k, dz, o : o + h] = both(i, o, h).astype(bf16)
            part = (slice(None), pl.ds(a, n))
            send(("bxf", q, k), xf_send.at[k].at[part], xf_recv.at[k].at[part], dict(dx=d))

    def back_z(q):
        a, n = BWD[q]
        recv(("bxf", q, 0))
        recv(("bxf", q, 1))
        for dz in (3, 1, 2, 0):
            total = both(dz * 4, a, n)
            total = total + xf_recv[0, dz, a : a + n].astype(f32) + xf_recv[1, dz, a : a + n].astype(f32)
            if dz:
                z_send[dz - 1, a : a + n] = total.astype(bf16)
                send(("bz", q, dz), z_send.at[dz - 1, pl.ds(a, n)], z_recv.at[dz - 1, pl.ds(a, n)], dict(dzh=STEP[dz]))
            else:
                comb[0, a : a + n] = total

    def back_last(q):
        a, n = BWD[q]
        total = comb[0, a : a + n]
        for dz in (1, 2, 3):
            recv(("bz", q, dz))
            total = total + z_recv[dz - 1, a : a + n].astype(f32)
        fg_t[a : a + n] = total

    weight_1()
    back_products(0)
    weight_2()
    back_xh(0)
    back_products(1)
    weight_3()
    back_xf(0)
    back_xh(1)
    back_products(2)
    weight_4()
    back_xf(1)
    back_z(0)
    back_xh(2)
    back_products(3)
    weight_5()
    back_xf(2)
    back_z(1)
    back_xh(3)
    weight_6()
    back_last(0)
    back_xf(3)
    weight_7()
    back_z(2)
    back_last(1)
    weight_8()
    back_z(3)
    back_last(2)
    back_last(3)
    fgrad_ref[...] = fg_t[...].T.astype(bf16)
    for copy in channels.values():
        copy.wait_send()


def per_device(features, tiles, tile_rows, tile_cols, tile_count, weight, cotangent):
    vmem = pl.BlockSpec(memory_space=pltpu.VMEM)
    smem = pl.BlockSpec(memory_space=pltpu.SMEM)
    square = lambda *lead: pltpu.VMEM((*lead, T, T), bf16)
    wide = lambda *shape: pltpu.VMEM(shape, f32)
    nmax = max(n for _, n in FWD + BWD)
    n_channels = 24 * len(FWD) + 6 * len(FWD) + 18 * len(BWD) + 24
    scratch = [
        square(SLOTS), square(SLOTS), wide(SLOTS, nmax, T), square(8), square(8), wide(T, T), square(), square(), square(),
        square(16), square(16), wide(16, T, T), square(4), square(4), square(2, 4), square(2, 4), square(3), square(3), wide(T, T),
        wide(T, T), wide(128, T), wide(128, T), wide(3, 32, T), wide(32, T), wide(3, 8, T), wide(8, 8, T), wide(32, T),
        wide(128, T), wide(T, T), pltpu.VMEM((8, 128), jnp.int32), pltpu.SMEM((8, 128), jnp.int32),
        pltpu.SemaphoreType.DMA((n_channels,)), pltpu.SemaphoreType.DMA((n_channels,)), pltpu.SemaphoreType.DMA((9,)),
    ]
    scratch += [pltpu.VMEM((32, n, T), bf16) for _, n in FWD]
    scratch += [pltpu.VMEM((8, n, T), bf16) for _, n in BWD]
    return pl.pallas_call(
        kernel,
        name="graph_layer",
        out_shape=(
            jax.ShapeDtypeStruct((T, T), bf16),
            jax.ShapeDtypeStruct((T, T), f32),
            jax.ShapeDtypeStruct((T, T), bf16),
        ),
        in_specs=[vmem, pl.BlockSpec(memory_space=pl.ANY), vmem, vmem, smem, vmem, vmem],
        out_specs=(vmem, vmem, vmem),
        scratch_shapes=scratch,
        compiler_params=pltpu.CompilerParams(
            collective_id=0, has_side_effects=True, vmem_limit_bytes=58 << 20
        ),
    )(
        features,
        tiles.reshape(SLOTS, T, T),
        tile_rows.reshape(1, SLOTS),
        tile_cols.reshape(1, SLOTS),
        tile_count.reshape(1, 1),
        weight,
        cotangent,
    )


def solution(mesh):
    placed = (
        P(("section", "rep"), None),
        P("section", "rep", None, None, None),
        P("section", "rep", None),
        P("section", "rep", None),
        P("section", "rep"),
        P(),
        P(("section", "rep"), None),
    )
    return jax.shard_map(
        per_device,
        mesh=mesh,
        in_specs=placed,
        out_specs=(P(("section", "rep"), None), P(), P(("section", "rep"), None)),
        check_vma=False,
    )
```

```python
import jax
import jax.numpy as jnp
from jax import lax
from jax.experimental import pallas as pl
from jax.experimental.pallas import tpu as pltpu
from jax.sharding import PartitionSpec as P

f32, bf16 = jnp.float32, jnp.bfloat16
T = 256
SLOTS = 64
STEP = (0, 1, -1, 2)
FWD = ((0, 64), (64, 64), (128, 64), (192, 64))
BWD = FWD
UNROLL = 16
ARRIVALS = 18 * len(FWD) + 7
DEPARTURES = 4 * len(FWD) + 7


def transpose(v):
    return v.T


def kernel(
    feat_ref, tiles_ref, rows_ref, cols_ref, count_ref, weight_ref, cot_ref,
    act_ref, wgrad_ref, fgrad_ref,
    tiles, tiles_t, prefix, rs_send, rs_recv, agg_own, agg_t, wt, cot_t,
    c_send, c_recv, comb, xh_send, xh_recv, xf_send, xf_recv, z_send, z_recv, fg_t,
    w0, w1r, w1, w2r, w2, w3r, w4, w5, w6, w7, table_v, table,
    send_sem, recv_sem, local_sem, *per_slice,
):
    gathered, row_grads = per_slice[: len(FWD)], per_slice[len(FWD) :]
    section, rep = lax.axis_index("section"), lax.axis_index("rep")
    zh, x, c = section // 8, (section // 2) % 4, section % 2
    zl, y = rep // 4, rep % 4

    def at(dzh=0, dx=0, dc=0, dzl=0, dy=0):
        return (
            (((zh + dzh + 4) % 4) * 4 + (x + dx + 4) % 4) * 2 + (c + dc) % 2,
            ((zl + dzl) % 2) * 4 + (y + dy + 4) % 4,
        )

    rep_offs = [dict(dzl=e // 4, dy=STEP[e % 4]) for e in range(8)]
    partners = (
        [dict(dx=STEP[i]) for i in (1, 2, 3)]
        + [dict(dzh=STEP[i]) for i in (1, 2, 3)]
        + [dict(dc=1)]
        + rep_offs[1:]
    )
    back = (0, 2, 1, 3)
    arrivals, departures = {}, {}

    def copy_of(src, dst, out, into, off):
        return pltpu.make_async_remote_copy(
            src_ref=src, dst_ref=dst, send_sem=send_sem.at[out], recv_sem=recv_sem.at[into],
            device_id=at(**off), device_id_type=pl.DeviceIdType.MESH,
        )

    def send(into, out, src, dst, off):
        i = arrivals.setdefault(into, len(arrivals))
        o = departures.setdefault(out, len(departures))
        copy_of(src, dst, o, i, off).start()

    def recv(into, ref):
        copy_of(ref, ref, 0, arrivals[into], dict(dx=1)).wait_recv()

    def sent(out, ref):
        copy_of(ref, ref, departures[out], 0, dict(dx=1)).wait_send()

    barrier = pltpu.get_barrier_semaphore()
    for off in partners:
        pl.semaphore_signal(barrier, inc=1, device_id=at(**off), device_id_type=pl.DeviceIdType.MESH)
    loads = [
        pltpu.make_async_copy(tiles_ref.at[pl.ds(i * 8, 8)], tiles.at[pl.ds(i * 8, 8)], local_sem.at[i])
        for i in range(8)
    ]
    for load in loads:
        load.start()
    feat_t = transpose(feat_ref[...])
    for q, (a, n) in enumerate(FWD):
        gathered[q][0] = feat_t[a : a + n]
    pl.semaphore_wait(barrier, len(partners))

    def x_full(q, dz):
        g = gathered[q]
        send(("xf", q, dz), ("fwd", q), g.at[dz * 4], g.at[dz * 4 + 2], dict(dx=1))
        send(("xf", q, dz), ("fwd", q), g.at[dz * 4], g.at[dz * 4 + 1], dict(dx=-1))

    def z_full(q):
        g = gathered[q]
        send(("zf", q, 1), ("fwd", q), g.at[0], g.at[8], dict(dzh=1))
        send(("zf", q, -1), ("fwd", q), g.at[0], g.at[4], dict(dzh=-1))

    z_full(0)
    x_full(0, 0)
    z_full(1)
    x_full(1, 0)
    x_full(2, 0)
    x_full(3, 0)

    def make_tables():
        lane = lax.broadcasted_iota(jnp.int32, (SLOTS, SLOTS), 1)
        sub = lax.broadcasted_iota(jnp.int32, (SLOTS, SLOTS), 0)
        count = count_ref[0, 0]
        r_l = jnp.broadcast_to(rows_ref[...], (SLOTS, SLOTS))
        c_l = jnp.broadcast_to(cols_ref[...], (SLOTS, SLOTS))
        r_s = r_l.astype(f32).T.astype(jnp.int32)
        c_s = c_l.astype(f32).T.astype(jnp.int32)
        live_s = sub < count
        lane_w = lax.broadcasted_iota(jnp.int32, (SLOTS, 128), 1)
        sub_w = lax.broadcasted_iota(jnp.int32, (SLOTS, 128), 0)

        def ring(delta):
            d = (delta + 8) % 4
            return jnp.where(d == 2, 3, jnp.where(d == 3, 2, d))

        def one(major_l, minor_l, major_s, minor_s, width, other, base):
            key_l = jnp.where(lane < count, major_l * width + minor_l, 1000 + lane)
            key_s = jnp.where(live_s, major_s * width + minor_s, 1000 + sub)
            before = key_l < key_s
            rank = jnp.sum(before.astype(f32), axis=1, keepdims=True)
            same = jnp.sum((before & (major_l == major_s)).astype(f32), axis=1, keepdims=True)
            hot = jnp.broadcast_to(rank, (SLOTS, 128)) == lane_w.astype(f32)
            first = jnp.broadcast_to((same == 0).astype(f32), (SLOTS, 128))

            def pick(v):
                return jnp.sum(jnp.where(hot, v, 0.0), axis=0, keepdims=True).astype(jnp.int32)

            major_w = jnp.broadcast_to(major_s[:, :1], (SLOTS, 128))
            live_w = sub_w < count
            upto = jnp.sum((live_w & (major_w <= lane_w)).astype(f32), axis=0, keepdims=True)
            equal = jnp.sum((live_w & (major_w == lane_w)).astype(f32), axis=0, keepdims=True)
            last = jnp.where(equal > 0, upto - 1.0, -1.0).astype(jnp.int32)
            table_v[base : base + 1, :] = pick(sub_w.astype(f32))
            table_v[base + 1 : base + 2, :] = pick(jnp.broadcast_to(other[:, :1].astype(f32), (SLOTS, 128)))
            table_v[base + 2 : base + 3, :] = pick(first)
            table_v[base + 3 : base + 4, :] = last

        where_col = ((c_s + c) % 2) * 16 + ring(c_s // 8 - zh) * 4 + ring((c_s // 2) % 4 - x)
        where_row = ((r_s // 4 + zl) % 2) * 4 + ring(r_s % 4 - y)
        one(r_l, c_l, r_s, c_s, 32, where_col, 0)
        one(c_l, r_l, c_s, r_s, 8, where_row, 4)

    make_tables()
    to_smem = pltpu.make_async_copy(table_v, table, local_sem.at[8])
    to_smem.start()
    for load in loads:
        load.wait()

    def turn(first, number):
        def step(i, carry):
            for u in range(4):
                k = first + i * 4 + u
                tiles_t[k] = transpose(tiles[k])
            return carry

        lax.fori_loop(0, number // 4, step, 0)

    def products(source, matrices, base, n):
        def step(i, total):
            for u in range(UNROLL):
                p = i * UNROLL + u
                keep = jnp.where(table[base + 2, p] == 1, 0.0, 1.0)
                s = jnp.clip(table[base + 1, p], 0, source.shape[0] - 1)
                k = jnp.clip(table[base, p], 0, SLOTS - 1)
                total = total * keep + jnp.dot(source[s], matrices[k], preferred_element_type=f32)
                prefix[p, :n] = total
            return total

        lax.fori_loop(0, SLOTS // UNROLL, step, jnp.zeros((n, T), f32))

    def group(base, index, n):
        last = table[base + 3, index]
        return prefix[jnp.clip(last, 0, SLOTS - 1), :n] * jnp.where(last >= 0, 1.0, 0.0)

    def stage_z(q):
        g, h = gathered[q], FWD[q][1] // 2
        recv(("zf", q, 1), g.at[8])
        send(("zh", q), ("fwd", q), g.at[8, pl.ds(0, h)], g.at[12, pl.ds(0, h)], dict(dzh=1))
        x_full(q, 2)
        recv(("zf", q, -1), g.at[4])
        send(("zh", q), ("fwd", q), g.at[4, pl.ds(h, h)], g.at[12, pl.ds(h, h)], dict(dzh=-1))
        x_full(q, 1)

    def stage_z_last(q):
        recv(("zh", q), gathered[q].at[12])
        x_full(q, 3)

    def stage_xh(q, dz):
        g, h = gathered[q], FWD[q][1] // 2
        recv(("xf", q, dz), g.at[pl.ds(dz * 4 + 1, 2)])
        send(("xh", q, dz), ("fwd", q), g.at[dz * 4 + 2, pl.ds(0, h)], g.at[dz * 4 + 3, pl.ds(0, h)], dict(dx=1))
        send(("xh", q, dz), ("fwd", q), g.at[dz * 4 + 1, pl.ds(h, h)], g.at[dz * 4 + 3, pl.ds(h, h)], dict(dx=-1))

    def stage_core(q):
        g = gathered[q]
        for dz in (0, 2, 1, 3):
            recv(("xh", q, dz), g.at[dz * 4 + 3])
            send(("core", q), ("fwd", q), g.at[pl.ds(dz * 4, 4)], g.at[pl.ds(16 + dz * 4, 4)], dict(dc=1))

    def stage_products(q):
        a, n = FWD[q]
        recv(("core", q), gathered[q].at[pl.ds(16, 16)])
        products(gathered[q], tiles_t, 0, n)
        for e in (7, 3, 6, 5, 2, 1, 4):
            owner = at(**rep_offs[e])[1]
            rs_send[e, a : a + n] = group(0, owner, n).astype(bf16)
            to = (e // 4) * 4 + back[e % 4]
            send(("rs", q), ("rs", q), rs_send.at[e, pl.ds(a, n)], rs_recv.at[to, pl.ds(a, n)], rep_offs[e])
        agg_own[a : a + n] = group(0, rep, n)

    turn(0, 16)
    z_full(2)
    stage_xh(0, 0)
    turn(16, 16)
    z_full(3)
    stage_z(0)
    stage_xh(1, 0)
    turn(32, 16)
    stage_z_last(0)
    stage_z(1)
    stage_xh(2, 0)
    stage_xh(0, 2)
    stage_xh(0, 1)
    turn(48, 16)
    stage_z(2)
    stage_xh(3, 0)
    stage_xh(1, 2)
    stage_xh(1, 1)
    stage_z_last(1)
    stage_xh(0, 3)
    stage_z(3)
    stage_xh(2, 2)
    stage_xh(2, 1)
    stage_z_last(2)
    stage_xh(1, 3)
    stage_core(0)
    stage_xh(3, 2)
    stage_xh(3, 1)
    stage_z_last(3)
    to_smem.wait()
    wt[...] = transpose(weight_ref[...])
    cot_t[...] = transpose(cot_ref[...])
    stage_xh(2, 3)
    stage_core(1)
    stage_products(0)
    stage_xh(3, 3)
    stage_core(2)
    stage_products(1)
    stage_core(3)
    stage_products(2)
    stage_products(3)

    for q, (a, n) in enumerate(FWD):
        recv(("rs", q), rs_recv.at[pl.ds(1, 7), pl.ds(a, n)])
        total = agg_own[a : a + n]
        for e in range(1, 8):
            total = total + rs_recv[e, a : a + n].astype(f32)
        agg_t[a : a + n] = total.astype(bf16)

    def spread(q):
        for e in (7, 3, 6, 5, 2, 1, 4):
            to = (e // 4) * 4 + back[e % 4]
            send(("ag", q), ("ag", q), row_grads[q].at[0], row_grads[q].at[to], rep_offs[e])

    pre = jnp.dot(wt[...], agg_t[...], preferred_element_type=f32)
    sigma = jax.nn.sigmoid(pre)
    pre_grad = (cot_t[...].astype(f32) * (sigma * (1.0 + pre * (1.0 - sigma)))).astype(bf16)
    for q, (a, n) in enumerate(BWD):
        row_grads[q][0] = jnp.dot(weight_ref[a : a + n], pre_grad, preferred_element_type=f32).astype(bf16)
        if q == 0:
            spread(0)
    act_ref[...] = (pre * sigma).T.astype(bf16)
    w0[...] = lax.dot_general(agg_t[...], pre_grad, (((1,), (1,)), ((), ())), preferred_element_type=f32)
    spread(1)

    def aligned(v, k):
        return pl.ds(pl.multiple_of(v * k, k), k)

    def weight_1():
        send("w1", "w1", w0.at[aligned(1 - c, 128)], w1r, dict(dc=1))

    def weight_2():
        recv("w1", w1r)
        w1[...] = w0[aligned(c, 128), :] + w1r[...]
        for i in (3, 1, 2):
            send("w2", "w2", w1.at[aligned((x + STEP[i] + 4) % 4, 32)], w2r.at[back[i] - 1], dict(dx=STEP[i]))

    def weight_3():
        total = w1[aligned(x, 32), :]
        recv("w2", w2r)
        for i in (1, 2, 3):
            total = total + w2r[i - 1]
        w2[...] = total
        for i in (3, 1, 2):
            send("w3", "w3", w2.at[aligned((zh + STEP[i] + 4) % 4, 8)], w3r.at[back[i] - 1], dict(dzh=STEP[i]))

    def weight_4():
        total = w2[aligned(zh, 8), :]
        recv("w3", w3r)
        for i in (1, 2, 3):
            total = total + w3r[i - 1]
        w4[rep] = total
        for e in range(1, 8):
            send("w4", "w4", w4.at[rep], w4.at[rep], rep_offs[e])

    def weight_5():
        recv("w4", w4.at[pl.ds(0, 7)])
        w5[aligned(zh, 8), :] = jnp.sum(w4[...], axis=0)
        for i in (3, 1, 2):
            send("w5", "w5", w5.at[aligned(zh, 8)], w5.at[aligned(zh, 8)], dict(dzh=STEP[i]))

    def weight_6():
        recv("w5", w5.at[pl.ds(0, 24)])
        w6[aligned(x, 32), :] = w5[...]
        for i in (3, 1, 2):
            send("w6", "w6", w6.at[aligned(x, 32)], w6.at[aligned(x, 32)], dict(dx=STEP[i]))

    def weight_7():
        recv("w6", w6.at[pl.ds(0, 96)])
        w7[aligned(c, 128), :] = w6[...]
        send("w7", "w7", w7.at[aligned(c, 128)], w7.at[aligned(c, 128)], dict(dc=1))

    def weight_8():
        recv("w7", w7.at[pl.ds(0, 128)])
        wgrad_ref[...] = w7[...]

    def back_products(q):
        a, n = BWD[q]
        recv(("ag", q), row_grads[q].at[pl.ds(1, 7)])
        if q + 2 < len(BWD):
            spread(q + 2)
        products(row_grads[q], tiles, 4, n)
        for dz in (3, 1, 2, 0):
            for dx in (3, 1, 2, 0):
                other = at(dzh=STEP[dz], dx=STEP[dx], dc=1)[0]
                c_send[dz * 4 + dx, a : a + n] = group(4, other, n).astype(bf16)
            part = (pl.ds(dz * 4, 4), pl.ds(a, n))
            send(("bc", q), ("bwd", q), c_send.at[part], c_recv.at[part], dict(dc=1))
        for dz in (3, 1, 2, 0):
            for dx in (3, 1, 2, 0):
                own = at(dzh=STEP[dz], dx=STEP[dx])[0]
                comb[dz * 4 + dx, a : a + n] = group(4, own, n)

    def both(i, a, n):
        return comb[i, a : a + n] + c_recv[i, a : a + n].astype(f32)

    def back_xh(q):
        a, n = BWD[q]
        h = n // 2
        recv(("bc", q), c_recv.at[:, pl.ds(a, n)])
        for dz in range(4):
            xh_send[dz, a : a + n] = both(dz * 4 + 3, a, n).astype(bf16)
        for k, d, s in ((0, 1, a), (1, -1, a + h)):
            send(("bxh", q), ("bwd", q), xh_send.at[:, pl.ds(s, h)], xh_recv.at[:, pl.ds(s, h)], dict(dx=d))

    def back_xf(q):
        a, n = BWD[q]
        h = n // 2
        recv(("bxh", q), xh_recv.at[:, pl.ds(a, n)])
        for k, d, s in ((0, 1, a), (1, -1, a + h)):
            o = a + h if k == 0 else a
            for dz in range(4):
                i = dz * 4 + 1 + k
                xf_send[k, dz, s : s + h] = (both(i, s, h) + xh_recv[dz, s : s + h].astype(f32)).astype(bf16)
                xf_send[k, dz, o : o + h] = both(i, o, h).astype(bf16)
            part = (slice(None), pl.ds(a, n))
            send(("bxf", q), ("bwd", q), xf_send.at[k].at[part], xf_recv.at[k].at[part], dict(dx=d))

    def back_z(q):
        a, n = BWD[q]
        recv(("bxf", q), xf_recv.at[:, :, pl.ds(a, n)])
        for dz in (3, 1, 2, 0):
            total = both(dz * 4, a, n)
            total = total + xf_recv[0, dz, a : a + n].astype(f32) + xf_recv[1, dz, a : a + n].astype(f32)
            if dz:
                z_send[dz - 1, a : a + n] = total.astype(bf16)
                send(("bz", q), ("bwd", q), z_send.at[dz - 1, pl.ds(a, n)], z_recv.at[dz - 1, pl.ds(a, n)], dict(dzh=STEP[dz]))
            else:
                comb[0, a : a + n] = total

    def back_last(q):
        a, n = BWD[q]
        total = comb[0, a : a + n]
        recv(("bz", q), z_recv.at[:, pl.ds(a, n)])
        for dz in (1, 2, 3):
            total = total + z_recv[dz - 1, a : a + n].astype(f32)
        fg_t[a : a + n] = total

    weight_1()
    back_products(0)
    weight_2()
    back_xh(0)
    back_products(1)
    weight_3()
    back_xh(1)
    back_xf(0)
    back_products(2)
    weight_4()
    back_xh(2)
    back_xf(1)
    back_products(3)
    weight_5()
    back_xh(3)
    back_z(0)
    back_xf(2)
    weight_6()
    back_z(1)
    back_xf(3)
    back_last(0)
    weight_7()
    back_z(2)
    back_last(1)
    weight_8()
    back_z(3)
    back_last(2)
    back_last(3)
    fgrad_ref[...] = fg_t[...].T.astype(bf16)
    for q, (a, n) in enumerate(FWD):
        sent(("fwd", q), gathered[q].at[pl.ds(0, 31)])
        sent(("rs", q), rs_send.at[pl.ds(1, 7), pl.ds(a, n)])
        sent(("ag", q), row_grads[q].at[pl.ds(1, 7)])
        sent(("bwd", q), gathered[q].at[pl.ds(0, 31)])
    for name, ref in (
        ("w1", w1r), ("w2", w2r), ("w3", w3r), ("w4", w4.at[pl.ds(0, 7)]),
        ("w5", w5.at[pl.ds(0, 24)]), ("w6", w6.at[pl.ds(0, 96)]), ("w7", w7.at[pl.ds(0, 128)]),
    ):
        sent(name, ref)
    assert len(arrivals) == ARRIVALS and len(departures) == DEPARTURES


def hand_over(a_in, b_in, c_in, a_out, b_out, c_out):
    a_out[...] = a_in[...]
    b_out[...] = b_in[...]
    c_out[...] = c_in[...]


def per_device(features, tiles, tile_rows, tile_cols, tile_count, weight, cotangent):
    vmem = pl.BlockSpec(memory_space=pltpu.VMEM)
    smem = pl.BlockSpec(memory_space=pltpu.SMEM)
    square = lambda *lead: pltpu.VMEM((*lead, T, T), bf16)
    wide = lambda *shape: pltpu.VMEM(shape, f32)
    nmax = max(n for _, n in FWD + BWD)
    scratch = [
        square(SLOTS), square(SLOTS), wide(SLOTS, nmax, T), square(8), square(8), wide(T, T), square(), square(), square(),
        square(16), square(16), wide(16, T, T), square(4), square(4), square(2, 4), square(2, 4), square(3), square(3), wide(T, T),
        wide(T, T), wide(128, T), wide(128, T), wide(3, 32, T), wide(32, T), wide(3, 8, T), wide(8, 8, T), wide(32, T),
        wide(128, T), wide(T, T), pltpu.VMEM((8, 128), jnp.int32), pltpu.SMEM((8, 128), jnp.int32),
        pltpu.SemaphoreType.DMA((DEPARTURES,)), pltpu.SemaphoreType.DMA((ARRIVALS,)), pltpu.SemaphoreType.DMA((9,)),
    ]
    scratch += [pltpu.VMEM((32, n, T), bf16) for _, n in FWD]
    scratch += [pltpu.VMEM((8, n, T), bf16) for _, n in BWD]
    results = pl.pallas_call(
        kernel,
        name="graph_layer",
        out_shape=(
            jax.ShapeDtypeStruct((T, T), bf16),
            jax.ShapeDtypeStruct((T, T), f32),
            jax.ShapeDtypeStruct((T, T), bf16),
        ),
        in_specs=[vmem, pl.BlockSpec(memory_space=pl.ANY), vmem, vmem, smem, vmem, vmem],
        out_specs=(vmem, vmem, vmem),
        scratch_shapes=scratch,
        compiler_params=pltpu.CompilerParams(
            collective_id=0, has_side_effects=True, vmem_limit_bytes=58 << 20
        ),
    )(
        features,
        tiles.reshape(SLOTS, T, T),
        tile_rows.reshape(1, SLOTS),
        tile_cols.reshape(1, SLOTS),
        tile_count.reshape(1, 1),
        weight,
        cotangent,
    )
    return pl.pallas_call(
        hand_over,
        name="hand_over",
        out_shape=tuple(jax.ShapeDtypeStruct(v.shape, v.dtype) for v in results),
        in_specs=[vmem] * 3,
        out_specs=(vmem,) * 3,
    )(*results)


def solution(mesh):
    placed = (
        P(("section", "rep"), None),
        P("section", "rep", None, None, None),
        P("section", "rep", None),
        P("section", "rep", None),
        P("section", "rep"),
        P(),
        P(("section", "rep"), None),
    )
    return jax.shard_map(
        per_device,
        mesh=mesh,
        in_specs=placed,
        out_specs=(P(("section", "rep"), None), P(), P(("section", "rep"), None)),
        check_vma=False,
    )
```

```python
import jax
import jax.numpy as jnp
from jax import lax
from jax.experimental import pallas as pl
from jax.experimental.pallas import tpu as pltpu
from jax.sharding import PartitionSpec as P

f32, bf16 = jnp.float32, jnp.bfloat16
T = 256
SLOTS = 64
STEP = (0, 1, -1, 2)
FWD = ((0, 64), (64, 64), (128, 64), (192, 64))
BWD = FWD
UNROLL = 16
ARRIVALS = 18 * len(FWD) + 7
DEPARTURES = 4 * len(FWD) + 7


def transpose(v):
    return v.T


def kernel(
    feat_ref, tiles_ref, rows_ref, cols_ref, count_ref, weight_ref, cot_ref,
    act_ref, wgrad_ref, fgrad_ref,
    tiles, tiles_t, prefix, rs_send, rs_recv, agg_own, agg_t, wt, cot_t,
    c_send, c_recv, comb, xh_send, xh_recv, xf_send, xf_recv, z_send, z_recv, fg_t,
    w0, w1r, w1, w2r, w2, w3r, w4, w5, w6, w7, table_v, table,
    send_sem, recv_sem, local_sem, *per_slice,
):
    gathered, row_grads = per_slice[: len(FWD)], per_slice[len(FWD) :]
    section, rep = lax.axis_index("section"), lax.axis_index("rep")
    zh, x, c = section // 8, (section // 2) % 4, section % 2
    zl, y = rep // 4, rep % 4

    def at(dzh=0, dx=0, dc=0, dzl=0, dy=0):
        return (
            (((zh + dzh + 4) % 4) * 4 + (x + dx + 4) % 4) * 2 + (c + dc) % 2,
            ((zl + dzl) % 2) * 4 + (y + dy + 4) % 4,
        )

    rep_offs = [dict(dzl=e // 4, dy=STEP[e % 4]) for e in range(8)]
    partners = (
        [dict(dx=STEP[i]) for i in (1, 2, 3)]
        + [dict(dzh=STEP[i]) for i in (1, 2, 3)]
        + [dict(dc=1)]
        + rep_offs[1:]
    )
    back = (0, 2, 1, 3)
    arrivals, departures = {}, {}

    def copy_of(src, dst, out, into, off):
        return pltpu.make_async_remote_copy(
            src_ref=src, dst_ref=dst, send_sem=send_sem.at[out], recv_sem=recv_sem.at[into],
            device_id=at(**off), device_id_type=pl.DeviceIdType.MESH,
        )

    def send(into, out, src, dst, off):
        i = arrivals.setdefault(into, len(arrivals))
        o = departures.setdefault(out, len(departures))
        copy_of(src, dst, o, i, off).start()

    def recv(into, ref):
        copy_of(ref, ref, 0, arrivals[into], dict(dx=1)).wait_recv()

    def sent(out, ref):
        copy_of(ref, ref, departures[out], 0, dict(dx=1)).wait_send()

    barrier = pltpu.get_barrier_semaphore()
    for off in partners:
        pl.semaphore_signal(barrier, inc=1, device_id=at(**off), device_id_type=pl.DeviceIdType.MESH)
    loads = [
        pltpu.make_async_copy(tiles_ref.at[pl.ds(i * 8, 8)], tiles.at[pl.ds(i * 8, 8)], local_sem.at[i])
        for i in range(8)
    ]
    for load in loads:
        load.start()
    feat_t = transpose(feat_ref[...])
    for q, (a, n) in enumerate(FWD):
        gathered[q][0] = feat_t[a : a + n]
    pl.semaphore_wait(barrier, len(partners))

    def x_full(q, dz):
        g = gathered[q]
        send(("xf", q, dz), ("fwd", q), g.at[dz * 4], g.at[dz * 4 + 2], dict(dx=1))
        send(("xf", q, dz), ("fwd", q), g.at[dz * 4], g.at[dz * 4 + 1], dict(dx=-1))

    def z_full(q):
        g = gathered[q]
        send(("zf", q, 1), ("fwd", q), g.at[0], g.at[8], dict(dzh=1))
        send(("zf", q, -1), ("fwd", q), g.at[0], g.at[4], dict(dzh=-1))

    z_full(0)
    x_full(0, 0)
    z_full(1)
    x_full(1, 0)
    x_full(2, 0)
    x_full(3, 0)

    def make_tables():
        lane = lax.broadcasted_iota(jnp.int32, (SLOTS, SLOTS), 1)
        sub = lax.broadcasted_iota(jnp.int32, (SLOTS, SLOTS), 0)
        count = count_ref[0, 0]
        r_l = jnp.broadcast_to(rows_ref[...], (SLOTS, SLOTS))
        c_l = jnp.broadcast_to(cols_ref[...], (SLOTS, SLOTS))
        r_s = r_l.astype(f32).T.astype(jnp.int32)
        c_s = c_l.astype(f32).T.astype(jnp.int32)
        live_s = sub < count
        lane_w = lax.broadcasted_iota(jnp.int32, (SLOTS, 128), 1)
        sub_w = lax.broadcasted_iota(jnp.int32, (SLOTS, 128), 0)

        def ring(delta):
            d = (delta + 8) % 4
            return jnp.where(d == 2, 3, jnp.where(d == 3, 2, d))

        def one(major_l, minor_l, major_s, minor_s, width, other, base):
            key_l = jnp.where(lane < count, major_l * width + minor_l, 1000 + lane)
            key_s = jnp.where(live_s, major_s * width + minor_s, 1000 + sub)
            before = key_l < key_s
            rank = jnp.sum(before.astype(f32), axis=1, keepdims=True)
            same = jnp.sum((before & (major_l == major_s)).astype(f32), axis=1, keepdims=True)
            hot = jnp.broadcast_to(rank, (SLOTS, 128)) == lane_w.astype(f32)
            first = jnp.broadcast_to((same == 0).astype(f32), (SLOTS, 128))

            def pick(v):
                return jnp.sum(jnp.where(hot, v, 0.0), axis=0, keepdims=True).astype(jnp.int32)

            major_w = jnp.broadcast_to(major_s[:, :1], (SLOTS, 128))
            live_w = sub_w < count
            upto = jnp.sum((live_w & (major_w <= lane_w)).astype(f32), axis=0, keepdims=True)
            equal = jnp.sum((live_w & (major_w == lane_w)).astype(f32), axis=0, keepdims=True)
            last = jnp.where(equal > 0, upto - 1.0, -1.0).astype(jnp.int32)
            table_v[base : base + 1, :] = pick(sub_w.astype(f32))
            table_v[base + 1 : base + 2, :] = pick(jnp.broadcast_to(other[:, :1].astype(f32), (SLOTS, 128)))
            table_v[base + 2 : base + 3, :] = pick(first)
            table_v[base + 3 : base + 4, :] = last

        where_col = ((c_s + c) % 2) * 16 + ring(c_s // 8 - zh) * 4 + ring((c_s // 2) % 4 - x)
        where_row = ((r_s // 4 + zl) % 2) * 4 + ring(r_s % 4 - y)
        one(r_l, c_l, r_s, c_s, 32, where_col, 0)
        one(c_l, r_l, c_s, r_s, 8, where_row, 4)

    make_tables()
    to_smem = pltpu.make_async_copy(table_v, table, local_sem.at[8])
    to_smem.start()
    for load in loads:
        load.wait()

    def turn(first, number):
        def step(i, carry):
            for u in range(4):
                k = first + i * 4 + u
                tiles_t[k] = transpose(tiles[k])
            return carry

        lax.fori_loop(0, number // 4, step, 0)

    def products(source, matrices, base, n):
        def step(i, total):
            for u in range(UNROLL):
                p = i * UNROLL + u
                keep = jnp.where(table[base + 2, p] == 1, 0.0, 1.0)
                s = jnp.clip(table[base + 1, p], 0, source.shape[0] - 1)
                k = jnp.clip(table[base, p], 0, SLOTS - 1)
                total = total * keep + jnp.dot(source[s], matrices[k], preferred_element_type=f32)
                prefix[p, :n] = total
            return total

        lax.fori_loop(0, SLOTS // UNROLL, step, jnp.zeros((n, T), f32))

    def group(base, index, n):
        last = table[base + 3, index]
        return prefix[jnp.clip(last, 0, SLOTS - 1), :n] * jnp.where(last >= 0, 1.0, 0.0)

    def stage_z(q):
        g, h = gathered[q], FWD[q][1] // 2
        recv(("zf", q, 1), g.at[8])
        send(("zh", q), ("fwd", q), g.at[8, pl.ds(0, h)], g.at[12, pl.ds(0, h)], dict(dzh=1))
        x_full(q, 2)
        recv(("zf", q, -1), g.at[4])
        send(("zh", q), ("fwd", q), g.at[4, pl.ds(h, h)], g.at[12, pl.ds(h, h)], dict(dzh=-1))
        x_full(q, 1)

    def stage_z_last(q):
        recv(("zh", q), gathered[q].at[12])
        x_full(q, 3)

    def stage_xh(q, dz):
        g, h = gathered[q], FWD[q][1] // 2
        recv(("xf", q, dz), g.at[pl.ds(dz * 4 + 1, 2)])
        send(("xh", q, dz), ("fwd", q), g.at[dz * 4 + 2, pl.ds(0, h)], g.at[dz * 4 + 3, pl.ds(0, h)], dict(dx=1))
        send(("xh", q, dz), ("fwd", q), g.at[dz * 4 + 1, pl.ds(h, h)], g.at[dz * 4 + 3, pl.ds(h, h)], dict(dx=-1))

    def stage_core(q):
        g = gathered[q]
        for dz in (0, 2, 1, 3):
            recv(("xh", q, dz), g.at[dz * 4 + 3])
            send(("core", q), ("fwd", q), g.at[pl.ds(dz * 4, 4)], g.at[pl.ds(16 + dz * 4, 4)], dict(dc=1))

    def stage_products(q):
        a, n = FWD[q]
        recv(("core", q), gathered[q].at[pl.ds(16, 16)])
        products(gathered[q], tiles_t, 0, n)
        for e in (7, 3, 6, 5, 2, 1, 4):
            owner = at(**rep_offs[e])[1]
            rs_send[e, a : a + n] = group(0, owner, n).astype(bf16)
            to = (e // 4) * 4 + back[e % 4]
            send(("rs", q), ("rs", q), rs_send.at[e, pl.ds(a, n)], rs_recv.at[to, pl.ds(a, n)], rep_offs[e])
        agg_own[a : a + n] = group(0, rep, n)

    z_full(2)
    turn(0, 32)
    stage_xh(0, 0)
    stage_z(0)
    z_full(3)
    stage_xh(1, 0)
    turn(32, 32)
    stage_z(1)
    stage_xh(2, 0)
    stage_xh(0, 2)
    stage_xh(0, 1)
    stage_z_last(0)
    stage_z(2)
    stage_xh(3, 0)
    stage_xh(1, 2)
    stage_xh(1, 1)
    stage_z_last(1)
    stage_xh(0, 3)
    stage_z(3)
    stage_xh(2, 2)
    stage_xh(2, 1)
    stage_z_last(2)
    stage_xh(1, 3)
    stage_core(0)
    stage_xh(3, 2)
    stage_xh(3, 1)
    stage_z_last(3)
    to_smem.wait()
    wt[...] = transpose(weight_ref[...])
    cot_t[...] = transpose(cot_ref[...])
    stage_xh(2, 3)
    stage_core(1)
    stage_products(0)
    stage_xh(3, 3)
    stage_core(2)
    stage_products(1)
    stage_core(3)
    stage_products(2)
    stage_products(3)

    for q, (a, n) in enumerate(FWD):
        recv(("rs", q), rs_recv.at[pl.ds(1, 7), pl.ds(a, n)])
        total = agg_own[a : a + n]
        for e in range(1, 8):
            total = total + rs_recv[e, a : a + n].astype(f32)
        agg_t[a : a + n] = total.astype(bf16)

    def spread(q):
        for e in (7, 3, 6, 5, 2, 1, 4):
            to = (e // 4) * 4 + back[e % 4]
            send(("ag", q), ("ag", q), row_grads[q].at[0], row_grads[q].at[to], rep_offs[e])

    pre = jnp.dot(wt[...], agg_t[...], preferred_element_type=f32)
    sigma = jax.nn.sigmoid(pre)
    pre_grad = (cot_t[...].astype(f32) * (sigma * (1.0 + pre * (1.0 - sigma)))).astype(bf16)
    for q, (a, n) in enumerate(BWD):
        row_grads[q][0] = jnp.dot(weight_ref[a : a + n], pre_grad, preferred_element_type=f32).astype(bf16)
        if q == 0:
            spread(0)
    act_ref[...] = (pre * sigma).T.astype(bf16)
    w0[...] = lax.dot_general(agg_t[...], pre_grad, (((1,), (1,)), ((), ())), preferred_element_type=f32)
    spread(1)

    def aligned(v, k):
        return pl.ds(pl.multiple_of(v * k, k), k)

    def weight_1():
        send("w1", "w1", w0.at[aligned(1 - c, 128)], w1r, dict(dc=1))

    def weight_2():
        recv("w1", w1r)
        w1[...] = w0[aligned(c, 128), :] + w1r[...]
        for i in (3, 1, 2):
            send("w2", "w2", w1.at[aligned((x + STEP[i] + 4) % 4, 32)], w2r.at[back[i] - 1], dict(dx=STEP[i]))

    def weight_3():
        total = w1[aligned(x, 32), :]
        recv("w2", w2r)
        for i in (1, 2, 3):
            total = total + w2r[i - 1]
        w2[...] = total
        for i in (3, 1, 2):
            send("w3", "w3", w2.at[aligned((zh + STEP[i] + 4) % 4, 8)], w3r.at[back[i] - 1], dict(dzh=STEP[i]))

    def weight_4():
        total = w2[aligned(zh, 8), :]
        recv("w3", w3r)
        for i in (1, 2, 3):
            total = total + w3r[i - 1]
        w4[rep] = total
        for e in range(1, 8):
            send("w4", "w4", w4.at[rep], w4.at[rep], rep_offs[e])

    def weight_5():
        recv("w4", w4.at[pl.ds(0, 7)])
        w5[aligned(zh, 8), :] = jnp.sum(w4[...], axis=0)
        for i in (3, 1, 2):
            send("w5", "w5", w5.at[aligned(zh, 8)], w5.at[aligned(zh, 8)], dict(dzh=STEP[i]))

    def weight_6():
        recv("w5", w5.at[pl.ds(0, 24)])
        w6[aligned(x, 32), :] = w5[...]
        for i in (3, 1, 2):
            send("w6", "w6", w6.at[aligned(x, 32)], w6.at[aligned(x, 32)], dict(dx=STEP[i]))

    def weight_7():
        recv("w6", w6.at[pl.ds(0, 96)])
        w7[aligned(c, 128), :] = w6[...]
        send("w7", "w7", w7.at[aligned(c, 128)], w7.at[aligned(c, 128)], dict(dc=1))

    def weight_8():
        recv("w7", w7.at[pl.ds(0, 128)])
        wgrad_ref[...] = w7[...]

    def back_products(q):
        a, n = BWD[q]
        recv(("ag", q), row_grads[q].at[pl.ds(1, 7)])
        if q + 2 < len(BWD):
            spread(q + 2)
        products(row_grads[q], tiles, 4, n)
        for dz in (3, 1, 2, 0):
            for dx in (3, 1, 2, 0):
                other = at(dzh=STEP[dz], dx=STEP[dx], dc=1)[0]
                c_send[dz * 4 + dx, a : a + n] = group(4, other, n).astype(bf16)
            part = (pl.ds(dz * 4, 4), pl.ds(a, n))
            send(("bc", q), ("bwd", q), c_send.at[part], c_recv.at[part], dict(dc=1))
        for dz in (3, 1, 2, 0):
            for dx in (3, 1, 2, 0):
                own = at(dzh=STEP[dz], dx=STEP[dx])[0]
                comb[dz * 4 + dx, a : a + n] = group(4, own, n)

    def both(i, a, n):
        return comb[i, a : a + n] + c_recv[i, a : a + n].astype(f32)

    def back_xh(q):
        a, n = BWD[q]
        h = n // 2
        recv(("bc", q), c_recv.at[:, pl.ds(a, n)])
        for dz in range(4):
            xh_send[dz, a : a + n] = both(dz * 4 + 3, a, n).astype(bf16)
        for k, d, s in ((0, 1, a), (1, -1, a + h)):
            send(("bxh", q), ("bwd", q), xh_send.at[:, pl.ds(s, h)], xh_recv.at[:, pl.ds(s, h)], dict(dx=d))

    def back_xf(q):
        a, n = BWD[q]
        h = n // 2
        recv(("bxh", q), xh_recv.at[:, pl.ds(a, n)])
        for k, d, s in ((0, 1, a), (1, -1, a + h)):
            o = a + h if k == 0 else a
            for dz in range(4):
                i = dz * 4 + 1 + k
                xf_send[k, dz, s : s + h] = (both(i, s, h) + xh_recv[dz, s : s + h].astype(f32)).astype(bf16)
                xf_send[k, dz, o : o + h] = both(i, o, h).astype(bf16)
            part = (slice(None), pl.ds(a, n))
            send(("bxf", q), ("bwd", q), xf_send.at[k].at[part], xf_recv.at[k].at[part], dict(dx=d))

    def back_z(q):
        a, n = BWD[q]
        recv(("bxf", q), xf_recv.at[:, :, pl.ds(a, n)])
        for dz in (3, 1, 2, 0):
            total = both(dz * 4, a, n)
            total = total + xf_recv[0, dz, a : a + n].astype(f32) + xf_recv[1, dz, a : a + n].astype(f32)
            if dz:
                z_send[dz - 1, a : a + n] = total.astype(bf16)
                send(("bz", q), ("bwd", q), z_send.at[dz - 1, pl.ds(a, n)], z_recv.at[dz - 1, pl.ds(a, n)], dict(dzh=STEP[dz]))
            else:
                comb[0, a : a + n] = total

    def back_last(q):
        a, n = BWD[q]
        total = comb[0, a : a + n]
        recv(("bz", q), z_recv.at[:, pl.ds(a, n)])
        for dz in (1, 2, 3):
            total = total + z_recv[dz - 1, a : a + n].astype(f32)
        fg_t[a : a + n] = total

    weight_1()
    back_products(0)
    weight_2()
    back_xh(0)
    back_products(1)
    weight_3()
    back_xh(1)
    back_xf(0)
    back_products(2)
    weight_4()
    back_xh(2)
    back_xf(1)
    back_products(3)
    weight_5()
    back_xh(3)
    back_z(0)
    back_xf(2)
    weight_6()
    back_z(1)
    back_xf(3)
    back_last(0)
    weight_7()
    back_z(2)
    back_last(1)
    weight_8()
    back_z(3)
    back_last(2)
    back_last(3)
    fgrad_ref[...] = fg_t[...].T.astype(bf16)
    for q, (a, n) in enumerate(FWD):
        sent(("fwd", q), gathered[q].at[pl.ds(0, 31)])
        sent(("rs", q), rs_send.at[pl.ds(1, 7), pl.ds(a, n)])
        sent(("ag", q), row_grads[q].at[pl.ds(1, 7)])
        sent(("bwd", q), gathered[q].at[pl.ds(0, 31)])
    for name, ref in (
        ("w1", w1r), ("w2", w2r), ("w3", w3r), ("w4", w4.at[pl.ds(0, 7)]),
        ("w5", w5.at[pl.ds(0, 24)]), ("w6", w6.at[pl.ds(0, 96)]), ("w7", w7.at[pl.ds(0, 128)]),
    ):
        sent(name, ref)
    assert len(arrivals) == ARRIVALS and len(departures) == DEPARTURES


def hand_over(a_in, b_in, c_in, a_out, b_out, c_out):
    a_out[...] = a_in[...]
    b_out[...] = b_in[...]
    c_out[...] = c_in[...]


def per_device(features, tiles, tile_rows, tile_cols, tile_count, weight, cotangent):
    vmem = pl.BlockSpec(memory_space=pltpu.VMEM)
    smem = pl.BlockSpec(memory_space=pltpu.SMEM)
    square = lambda *lead: pltpu.VMEM((*lead, T, T), bf16)
    wide = lambda *shape: pltpu.VMEM(shape, f32)
    nmax = max(n for _, n in FWD + BWD)
    scratch = [
        square(SLOTS), square(SLOTS), wide(SLOTS, nmax, T), square(8), square(8), wide(T, T), square(), square(), square(),
        square(16), square(16), wide(16, T, T), square(4), square(4), square(2, 4), square(2, 4), square(3), square(3), wide(T, T),
        wide(T, T), wide(128, T), wide(128, T), wide(3, 32, T), wide(32, T), wide(3, 8, T), wide(8, 8, T), wide(32, T),
        wide(128, T), wide(T, T), pltpu.VMEM((8, 128), jnp.int32), pltpu.SMEM((8, 128), jnp.int32),
        pltpu.SemaphoreType.DMA((DEPARTURES,)), pltpu.SemaphoreType.DMA((ARRIVALS,)), pltpu.SemaphoreType.DMA((9,)),
    ]
    scratch += [pltpu.VMEM((32, n, T), bf16) for _, n in FWD]
    scratch += [pltpu.VMEM((8, n, T), bf16) for _, n in BWD]
    results = pl.pallas_call(
        kernel,
        name="graph_layer",
        out_shape=(
            jax.ShapeDtypeStruct((T, T), bf16),
            jax.ShapeDtypeStruct((T, T), f32),
            jax.ShapeDtypeStruct((T, T), bf16),
        ),
        in_specs=[vmem, pl.BlockSpec(memory_space=pl.ANY), vmem, vmem, smem, vmem, vmem],
        out_specs=(vmem, vmem, vmem),
        scratch_shapes=scratch,
        compiler_params=pltpu.CompilerParams(
            collective_id=0, has_side_effects=True, vmem_limit_bytes=58 << 20
        ),
    )(
        features,
        tiles.reshape(SLOTS, T, T),
        tile_rows.reshape(1, SLOTS),
        tile_cols.reshape(1, SLOTS),
        tile_count.reshape(1, 1),
        weight,
        cotangent,
    )
    return pl.pallas_call(
        hand_over,
        name="hand_over",
        out_shape=tuple(jax.ShapeDtypeStruct(v.shape, v.dtype) for v in results),
        in_specs=[vmem] * 3,
        out_specs=(vmem,) * 3,
    )(*results)


def solution(mesh):
    placed = (
        P(("section", "rep"), None),
        P("section", "rep", None, None, None),
        P("section", "rep", None),
        P("section", "rep", None),
        P("section", "rep"),
        P(),
        P(("section", "rep"), None),
    )
    return jax.shard_map(
        per_device,
        mesh=mesh,
        in_specs=placed,
        out_specs=(P(("section", "rep"), None), P(), P(("section", "rep"), None)),
        check_vma=False,
    )
```
